32 devices in a mesh: groups: 2 (over x), band: 16 (over z, y, core).
Axes of the slice: x: 2, y: 2, z: 4, core: 2. Of those that a mesh axis runs over, the one named last changes fastest.
Arguments:
- state: float32 [83, 65536], P(None, ('groups', 'band')), parts along dimension 1, may hold values from -36 to 36
- mesh_latent: bfloat16 [65536, 512], P(('groups', 'band')), parts along dimension 0, may hold values from -6 to 6
- m2g_src: int32 [65536, 3], P(('groups', 'band')), parts along dimension 0, may hold values from 0 to 32767, as said below
- g2m_owner: int32 [65536, 1], P(('groups', 'band')), parts along dimension 0, may hold values from 0 to 15, as said below
- g2m_node: int32 [65536, 1], P(('groups', 'band')), parts along dimension 0, may hold values from 0 to 2047
- mesh_src: int32 [65536, 6], P(('groups', 'band')), parts along dimension 0, may hold values from 0 to 32767, as said below
- norm_gain: float32 [83], replicated, may hold values from 0.1 to 1.9
- w_dec_mesh: bfloat16 [512, 512], replicated, may hold values from -0.25 to 0.25
- w_dec_grid: bfloat16 [83, 512], replicated, may hold values from -0.625 to 0.625
- w_dec_out: bfloat16 [512, 83], replicated, may hold values from -0.15625 to 0.15625
- w_enc: bfloat16 [83, 512], replicated, may hold values from -0.625 to 0.625
- w_enc_out: bfloat16 [512, 512], replicated, may hold values from -0.125 to 0.125
- w_proc_src: bfloat16 [512, 512], replicated, may hold values from -0.25 to 0.25
- w_proc_dst: bfloat16 [512, 512], replicated, may hold values from -0.25 to 0.25
- w_proc_out: bfloat16 [512, 512], replicated, may hold values from -0.109375 to 0.109375
Outputs:
- new_state: float32 [83, 65536], P(None, ('groups', 'band')), parts along dimension 1
- mesh_out: bfloat16 [65536, 512], P(('groups', 'band')), parts along dimension 0
The draws below stay inside these ranges and needn't reach their ends.
There are 2 independent parts, one for each index of `groups`. The reference program is written for one: setup_inputs(seed, part) draws one part's arguments, and reference() takes and returns one part's arrays. A program takes and returns all parts, laid end to end along the dimension named above; an argument that names none is the same for every part. Nothing has to cross between parts.
Inputs may be any that keep to these rules, and one draw needn't show every extreme that they name: `m2g_src`: grid point g lies in band b = g // 2048; its senders lie from b * 2048 - 128 to (b + 1) * 2048 + 127, clipped to the mesh, and both ends are named in every band. `mesh_src`: mesh node m lies in patch b = m // 2048; its senders lie from b * 2048 - 128 to (b + 1) * 2048 + 127, clipped to the mesh, and both ends are named in every patch. `g2m_owner`: A grid point of band b names patch b, b - 1 or b + 1. Rows naming b - 1 lie among the band's first 256 rows, rows naming b + 1 among its last 256; each neighbour is named at most 128 times by one band, and exactly 128 times by every band of the first and last eighth of the bands (at least one band at each end) for each neighbour it has.
All inputs are finite; a program needn't handle non-finite values.
Results may differ from the reference program's by a relative error of at most 0.0056.
Values may be sent and summed in bfloat16 or wider, within the bound.
A program may use at most 128 MiB of HBM per device.

```python
import math
import jax
import jax.numpy as jnp
from jax import lax

C = 83
L = 512
GRID_DEV = 2048
MESH_DEV = 2048
HALO = 128
KD = 3
KN = 6
GRID = 32768
MESH = 32768
CAP = 128


def banded_sources(key, total_rows, block_rows, fanout):
    owner_band = jnp.arange(total_rows, dtype=jnp.int32) // block_rows
    lowest = jnp.maximum(owner_band * MESH_DEV - HALO, 0)
    highest = jnp.minimum((owner_band + 1) * MESH_DEV + HALO, MESH)
    raw_bits = jax.random.randint(key, (total_rows, fanout), 0, 1 << 20, dtype=jnp.int32)
    chosen = lowest[:, None] + raw_bits % (highest - lowest)[:, None]
    within = jnp.arange(total_rows, dtype=jnp.int32) % block_rows
    first_row = within == 0
    last_row = within == block_rows - 1
    column = jnp.where(first_row, lowest, jnp.where(last_row, highest - 1, chosen[:, 0]))
    return chosen.at[:, 0].set(column).astype(jnp.int32)


def draw_state(key, part):
    key = jax.random.fold_in(key, 11)
    first_key, second_key, third_key = jax.random.split(key, 3)
    channel_scale = jnp.exp(jax.random.uniform(first_key, (C, 1), jnp.float32, math.log(0.3), math.log(3.0)))
    point_scale = jnp.exp(jax.random.uniform(second_key, (1, GRID), jnp.float32, math.log(0.3), math.log(3.0)))
    fluctuation = jnp.clip(jax.random.normal(third_key, (C, GRID), jnp.float32), -4.0, 4.0)
    return (fluctuation * channel_scale * point_scale).astype(jnp.float32)


def draw_m2g_src(key, part):
    key = jax.random.fold_in(key, 23)
    return banded_sources(key, GRID, GRID_DEV, KD)


def draw_mesh_src(key, part):
    key = jax.random.fold_in(key, 37)
    return banded_sources(key, MESH, MESH_DEV, KN)


def draw_g2m_owner(key, part):
    key = jax.random.fold_in(key, 47)
    count_key, left_key, right_key = jax.random.split(key, 3)
    bands = GRID // GRID_DEV
    band_ids = jnp.arange(bands, dtype=jnp.int32)
    polar_width = max(bands // 8, 1)
    polar = (band_ids < polar_width) | (band_ids >= bands - polar_width)
    drawn = jax.random.randint(count_key, (bands, 2), CAP // 4, CAP, dtype=jnp.int32)
    counts = jnp.where(polar[:, None], CAP, drawn)
    left_count = jnp.where(band_ids > 0, counts[:, 0], 0)
    right_count = jnp.where(band_ids < bands - 1, counts[:, 1], 0)
    window = 2 * CAP
    left_perm = jax.vmap(lambda k: jax.random.permutation(k, window))(jax.random.split(left_key, bands)).astype(jnp.int32)
    right_perm = jax.vmap(lambda k: jax.random.permutation(k, window))(jax.random.split(right_key, bands)).astype(jnp.int32)
    within = jnp.arange(GRID_DEV, dtype=jnp.int32)
    front_index = jnp.minimum(within, window - 1)
    back_index = jnp.maximum(within - (GRID_DEV - window), 0)
    go_left = (within[None, :] < window) & (left_perm[:, front_index] < left_count[:, None])
    go_right = (within[None, :] >= GRID_DEV - window) & (right_perm[:, back_index] < right_count[:, None])
    owner = band_ids[:, None] - go_left.astype(jnp.int32) + go_right.astype(jnp.int32)
    return owner.reshape(GRID, 1).astype(jnp.int32)


def plant(values, own_key, smallest, top_value):
    extent = values.shape
    index_at = [jax.random.randint(jax.random.fold_in(own_key, axis), (), 0, extent[axis]) for axis in range(len(extent))]
    values = values.at[tuple(index_at)].set(smallest)
    longest = extent.index(max(extent))
    index_at[longest] = (index_at[longest] + 1) % extent[longest]
    return values.at[tuple(index_at)].set(top_value)


def shard_levels(own_key, dims, shards, low, high):
    loudness = 1.0
    for axis_at, shards_of in shards:
        draws = jax.random.uniform(jax.random.fold_in(jax.random.fold_in(own_key, 6), axis_at), (shards_of,), jnp.float32, low / len(shards), high / len(shards))
        loudness = loudness * jnp.repeat(jnp.exp(draws), dims[axis_at] // shards_of).reshape((-1,) + (1,) * (len(dims) - 1 - axis_at))
    return loudness


def bell_draw(rng, shape, deviation, limit, cuts=(), kind=jnp.bfloat16):
    result = jax.random.normal(rng, shape, jnp.float32) * deviation
    if len(cuts) > 0:
        result = shard_levels(rng, shape, cuts, -0.22, 0.18) * result
    return jnp.clip(result, min=-limit, max=limit).astype(kind)


def setup_inputs(seed: int = 0, part: int = 0) -> dict:
    arg_keys = jax.random.split(jax.random.key(seed), 16)
    own_keys = jax.random.split(jax.random.fold_in(arg_keys[15], part), 16)
    state = draw_state(jax.random.fold_in(jax.random.fold_in(arg_keys[15], part), 71), part)
    mesh_latent = bell_draw(own_keys[1], (MESH, L), 1.0, 6.0, ((0, 16),))
    m2g_src = draw_m2g_src(jax.random.fold_in(jax.random.fold_in(arg_keys[15], part), 71), part)
    g2m_owner = draw_g2m_owner(jax.random.fold_in(jax.random.fold_in(arg_keys[15], part), 71), part)
    g2m_node = plant(jax.random.randint(own_keys[4], (GRID, 1), 0, MESH_DEV), jax.random.fold_in(own_keys[4], 1), 0, MESH_DEV - 1).astype(jnp.int32)
    mesh_src = draw_mesh_src(jax.random.fold_in(jax.random.fold_in(arg_keys[15], part), 71), part)
    norm_gain = jnp.clip(1.0 + 0.18 * jax.random.normal(arg_keys[6], (C,), jnp.float32), 0.1, 1.9)
    w_dec_mesh = bell_draw(arg_keys[7], (L, L), L ** -0.5, 0.25)
    w_dec_grid = bell_draw(arg_keys[8], (C, L), C ** -0.5, 0.625)
    w_dec_out = bell_draw(arg_keys[9], (L, C), (KD * L) ** -0.5, 0.15625)
    w_enc = bell_draw(arg_keys[10], (C, L), C ** -0.5, 0.625)
    w_enc_out = bell_draw(arg_keys[11], (L, L), (4 * L) ** -0.5, 0.125)
    w_proc_src = bell_draw(arg_keys[12], (L, L), L ** -0.5, 0.25)
    w_proc_dst = bell_draw(arg_keys[13], (L, L), L ** -0.5, 0.25)
    w_proc_out = bell_draw(arg_keys[14], (L, L), (KN * L) ** -0.5, 0.109375)
    return dict(state=state, mesh_latent=mesh_latent, m2g_src=m2g_src, g2m_owner=g2m_owner, g2m_node=g2m_node, mesh_src=mesh_src, norm_gain=norm_gain, w_dec_mesh=w_dec_mesh, w_dec_grid=w_dec_grid, w_dec_out=w_dec_out, w_enc=w_enc, w_enc_out=w_enc_out, w_proc_src=w_proc_src, w_proc_dst=w_proc_dst, w_proc_out=w_proc_out)


def contract_first(left, right):
    return lax.dot_general(left, right, (((0,), (0,)), ((), ())), preferred_element_type=jnp.float32)

def silu_sum(source_table, positions, baseline, fanout):
    summed = jnp.zeros(baseline.shape, jnp.float32)
    for neighbour in range(fanout):
        picked = jnp.take(source_table, positions[:, neighbour], axis=0).astype(jnp.float32)
        summed = summed + jax.nn.silu(picked + baseline)
    return summed

def reference(state, mesh_latent, m2g_src, g2m_owner, g2m_node, mesh_src, norm_gain, w_dec_mesh, w_dec_grid, w_dec_out, w_enc, w_enc_out, w_proc_src, w_proc_dst, w_proc_out):
    projected = jnp.dot(mesh_latent, w_dec_mesh, preferred_element_type=jnp.float32).astype(jnp.bfloat16)
    grid_half = state.astype(jnp.bfloat16)
    bands = GRID // GRID_DEV

    def decode(band_index):
        band_rows = lax.dynamic_slice_in_dim(grid_half, band_index * GRID_DEV, GRID_DEV, 1)
        sources = lax.dynamic_slice_in_dim(m2g_src, band_index * GRID_DEV, GRID_DEV, 0)
        receiver = contract_first(band_rows, w_dec_grid)
        decoded = silu_sum(projected, sources, receiver, KD).astype(jnp.bfloat16)
        return lax.dot_general(w_dec_out, decoded, (((0,), (1,)), ((), ())), preferred_element_type=jnp.float32)
    update = lax.map(decode, jnp.arange(bands, dtype=jnp.int32))
    update = jnp.moveaxis(update, 0, 1).reshape(C, GRID)
    new_state = state + update
    average = lax.optimization_barrier(jnp.mean(new_state, axis=0, keepdims=True))
    centered = new_state - average
    variance = lax.optimization_barrier(jnp.mean(centered * centered, axis=0, keepdims=True))
    normed = (centered * lax.rsqrt(variance + 1e-05) * norm_gain[:, None]).astype(jnp.bfloat16)
    targets = (g2m_owner[:, 0] * MESH_DEV + g2m_node[:, 0]).astype(jnp.int32)

    def encode(collected, band_index):
        band_rows = lax.dynamic_slice_in_dim(normed, band_index * GRID_DEV, GRID_DEV, 1)
        band_targets = lax.dynamic_slice_in_dim(targets, band_index * GRID_DEV, GRID_DEV, 0)
        message = jax.nn.silu(contract_first(band_rows, w_enc)).astype(jnp.bfloat16)
        return (collected.at[band_targets].add(message.astype(jnp.float32)), None)
    collected, unused = lax.scan(encode, jnp.zeros((MESH, L), jnp.float32), jnp.arange(bands, dtype=jnp.int32))
    encoded = collected.astype(jnp.bfloat16)
    mesh_mid = (mesh_latent.astype(jnp.float32) + jnp.dot(encoded, w_enc_out, preferred_element_type=jnp.float32)).astype(jnp.bfloat16)
    sender = jnp.dot(mesh_mid, w_proc_src, preferred_element_type=jnp.float32).astype(jnp.bfloat16)
    own = jnp.dot(mesh_mid, w_proc_dst, preferred_element_type=jnp.float32)
    edges_sum = silu_sum(sender, mesh_src, own, KN).astype(jnp.bfloat16)
    mesh_out = (mesh_mid.astype(jnp.float32) + jnp.dot(edges_sum, w_proc_out, preferred_element_type=jnp.float32)).astype(jnp.bfloat16)
    return (new_state, mesh_out)
```

```python
import functools

import jax
import jax.numpy as jnp
from jax import lax
from jax.experimental import pallas as pl
from jax.experimental.pallas import tpu as pltpu
from jax.sharding import PartitionSpec as P

HALO = 128
KD = 3
KN = 6
BLOCK = 256
UNROLL = 8
PAD = 8


def dot(left, right, left_dim=1, right_dim=0):
    return lax.dot_general(
        left, right, (((left_dim,), (right_dim,)), ((), ())), preferred_element_type=jnp.float32
    )


def half_silu(half):
    return half * jnp.tanh(half) + half


def put_rows(table, first, values):
    count = values.shape[0]
    for part in range(values.shape[1] // 128):
        table[pl.ds(first + part, count, stride=4), :] = values[:, part * 128 : part * 128 + 128]


def get_rows(table, first, count):
    return jnp.concatenate(
        [table[pl.ds(first + part, count, stride=4), :] for part in range(4)], axis=1
    )


def gather_sum(table, index, rows, fanout, base, total, first):
    upper = lax.broadcasted_iota(jnp.int32, (8, 128), 0) >= 4

    def body(step, carry):
        for inner in range(UNROLL):
            pair = step * UNROLL + inner
            point = first + 2 * pair
            spot = pl.ds(pl.multiple_of(pair * 8, 8), 8)
            own = base[spot, :]
            summed = None
            for edge in range(fanout):
                left = table[pl.ds(index[edge * rows + point], 8), :]
                right = table[pl.ds(index[edge * rows + point + 1], 8), :]
                term = half_silu(jnp.where(upper, right, left) + own)
                summed = term if summed is None else summed + term
            total[spot, :] = summed
        return carry

    lax.fori_loop(0, BLOCK // 2 // UNROLL, body, 0)


def one_hot(ids, first):
    rows = lax.broadcasted_iota(jnp.int32, (BLOCK, ids.shape[1]), 0) + first
    return jnp.where(rows == ids, 1.0, 0.0).astype(jnp.bfloat16)


def kernel(
    bands,
    m2g_index,
    mesh_index,
    state,
    latent,
    local_ids,
    lower_ids,
    upper_ids,
    gain,
    w_dec_mesh,
    w_dec_grid,
    w_dec_out,
    w_enc,
    w_enc_out,
    w_proc_src,
    w_proc_dst,
    w_proc_out,
    new_state,
    mesh_out,
    table,
    base,
    total,
    message,
    collected,
    middle,
    halo_out,
    halo_in,
    halo_in2,
    rim,
    rim_ids,
    send_sem,
    recv_sem,
):
    me = lax.axis_index("band")
    rows = latent.shape[0]
    points = state.shape[1]
    blocks = rows // BLOCK
    has = (me > 0, me < bands - 1)
    other = (me - 1, me + 1)

    def copy(number, side, source, target):
        return pltpu.make_async_remote_copy(
            src_ref=source,
            dst_ref=target,
            send_sem=send_sem.at[2 * number + side],
            recv_sem=recv_sem.at[2 * number + side],
            device_id={"band": other[side]},
            device_id_type=pl.DeviceIdType.MESH,
        )

    def halo_copy(number, side, landing):
        return copy(number, side, halo_out.at[number // 3, side], landing.at[1 - side])

    def ids_copy(side):
        return copy(1, side, (lower_ids, upper_ids)[side], rim_ids.at[1 - side])

    def rim_copy(side):
        start = 0 if side == 0 else points - BLOCK
        return copy(
            2, side, message.at[pl.ds(start, BLOCK)], rim.at[pl.ds((1 - side) * BLOCK, BLOCK)]
        )

    def start(make):
        for side in (0, 1):

            @pl.when(has[side])
            def _():
                make(side).start()

    def finish(make):
        for side in (0, 1):

            @pl.when(has[side])
            def _():
                make(side).wait_send()

            @pl.when(has[1 - side])
            def _():
                make(side).wait_recv()

    proj_copy = functools.partial(halo_copy, 0, landing=halo_in)
    send_copy = functools.partial(halo_copy, 3, landing=halo_in2)

    def block_of(step):
        return jnp.where(step == 0, 0, jnp.where(step == 1, blocks - 1, step - 1))

    def unpack(landing):
        for side in (0, 1):
            first = PAD + side * 4 * (HALO + rows)

            @pl.when(has[side])
            def _():
                put_rows(table, first, 0.5 * landing[side].astype(jnp.float32))

    def fill_block(step, source, weight, number):
        block = block_of(step)
        row = pl.multiple_of(block * BLOCK, BLOCK)
        values = dot(source[pl.ds(row, BLOCK), :], weight[...])
        put_rows(table, PAD + 4 * (HALO + row), 0.5 * values)
        return values

    barrier = pltpu.get_barrier_semaphore()
    for side in (0, 1):

        @pl.when(has[side])
        def _():
            pl.semaphore_signal(
                barrier,
                inc=1,
                device_id={"band": other[side]},
                device_id_type=pl.DeviceIdType.MESH,
            )

    pl.semaphore_wait(barrier, jnp.where(me > 0, 1, 0) + jnp.where(me < bands - 1, 1, 0))

    for side in (0, 1):

        @pl.when(jnp.logical_not(has[side]))
        def _():
            first = PAD + side * 4 * (HALO + rows)
            table[pl.ds(first, 4 * HALO), :] = jnp.zeros((4 * HALO, 128), jnp.float32)
            rim[pl.ds(side * BLOCK, BLOCK), :] = jnp.zeros((BLOCK, rim.shape[1]), rim.dtype)
            rim_ids[side] = jnp.full((1, BLOCK), -1, jnp.int32)

    start(ids_copy)

    def project(step, carry):
        values = fill_block(step, latent, w_dec_mesh, 0)

        @pl.when(step == 0)
        def _():
            halo_out[0, 0] = values[:HALO].astype(jnp.bfloat16)

        @pl.when(step == 1)
        def _():
            halo_out[0, 1] = values[BLOCK - HALO :].astype(jnp.bfloat16)
            start(proj_copy)

        return carry

    lax.fori_loop(0, blocks, project, 0)
    finish(proj_copy)
    unpack(halo_in)

    def decode(step, carry):
        block = block_of(step)
        point = pl.multiple_of(block * BLOCK, BLOCK)
        columns = pl.ds(point, BLOCK)
        cells = state[:, columns]
        put_rows(base, 0, 0.5 * dot(cells.astype(jnp.bfloat16), w_dec_grid[...], 0, 0))
        gather_sum(table, m2g_index, points, KD, base, total, point)
        decoded = get_rows(total, 0, BLOCK).astype(jnp.bfloat16)
        fresh = cells + dot(w_dec_out[...], decoded, 1, 1)
        new_state[:, columns] = fresh
        average = jnp.mean(fresh, axis=0, keepdims=True)
        centered = fresh - average
        variance = jnp.mean(centered * centered, axis=0, keepdims=True)
        normed = (centered * lax.rsqrt(variance + 1e-05) * gain[...]).astype(jnp.bfloat16)
        sent = half_silu(0.5 * dot(normed, w_enc[...], 0, 0))
        message[columns, :] = sent.astype(jnp.bfloat16)

        @pl.when(step == 1)
        def _():
            start(rim_copy)

        return carry

    lax.fori_loop(0, points // BLOCK, decode, 0)

    def collect(block, carry):
        row = pl.multiple_of(block * BLOCK, BLOCK)
        collected[pl.ds(row, BLOCK), :] = dot(one_hot(local_ids[...], row), message[...])
        return carry

    lax.fori_loop(0, blocks, collect, 0)
    finish(ids_copy)
    finish(rim_copy)

    def update(step, carry):
        block = block_of(step)
        row = pl.multiple_of(block * BLOCK, BLOCK)
        span = pl.ds(row, BLOCK)
        encoded = collected[span, :]
        for side in (0, 1):
            encoded += dot(one_hot(rim_ids[side], row), rim[pl.ds(side * BLOCK, BLOCK), :])
        mixed = latent[span, :].astype(jnp.float32) + dot(
            encoded.astype(jnp.bfloat16), w_enc_out[...]
        )
        middle[span, :] = mixed.astype(jnp.bfloat16)
        values = fill_block(step, middle, w_proc_src, 1)

        @pl.when(step == 0)
        def _():
            halo_out[1, 0] = values[:HALO].astype(jnp.bfloat16)

        @pl.when(step == 1)
        def _():
            halo_out[1, 1] = values[BLOCK - HALO :].astype(jnp.bfloat16)
            start(send_copy)

        return carry

    lax.fori_loop(0, blocks, update, 0)
    finish(send_copy)
    unpack(halo_in2)

    def process(block, carry):
        row = pl.multiple_of(block * BLOCK, BLOCK)
        span = pl.ds(row, BLOCK)
        kept = middle[span, :]
        put_rows(base, 0, 0.5 * dot(kept, w_proc_dst[...]))
        gather_sum(table, mesh_index, rows, KN, base, total, row)
        edges = get_rows(total, 0, BLOCK).astype(jnp.bfloat16)
        result = kept.astype(jnp.float32) + dot(edges, w_proc_out[...])
        mesh_out[span, :] = result.astype(jnp.bfloat16)
        return carry

    lax.fori_loop(0, blocks, process, 0)


def shards(
    bands,
    state,
    mesh_latent,
    m2g_src,
    g2m_owner,
    g2m_node,
    mesh_src,
    norm_gain,
    w_dec_mesh,
    w_dec_grid,
    w_dec_out,
    w_enc,
    w_enc_out,
    w_proc_src,
    w_proc_dst,
    w_proc_out,
):
    position = lax.axis_index("band")
    rows, width = mesh_latent.shape
    points = state.shape[1]

    def places(sources):
        count = sources.shape[0]
        parity = lax.broadcasted_iota(jnp.int32, (1, count), 1) % 2
        local = sources.T - (position * rows - HALO)
        return (4 * local + (PAD - 4 * parity)).reshape(-1)

    relative = g2m_owner.T - position
    nodes = g2m_node.T
    local_ids = jnp.where(relative == 0, nodes, -1)
    lower_ids = jnp.where(relative[:, :BLOCK] == -1, nodes[:, :BLOCK], -1)
    upper_ids = jnp.where(relative[:, points - BLOCK :] == 1, nodes[:, points - BLOCK :], -1)
    vmem = pl.BlockSpec(memory_space=pltpu.VMEM)
    smem = pl.BlockSpec(memory_space=pltpu.SMEM)
    return pl.pallas_call(
        functools.partial(kernel, bands),
        out_shape=(
            jax.ShapeDtypeStruct(state.shape, jnp.float32),
            jax.ShapeDtypeStruct(mesh_latent.shape, jnp.bfloat16),
        ),
        in_specs=[smem, smem] + [vmem] * 14,
        out_specs=(vmem, vmem),
        scratch_shapes=[
            pltpu.VMEM((PAD + 4 * (rows + 2 * HALO) + 8, 128), jnp.float32),
            pltpu.VMEM((4 * BLOCK, 128), jnp.float32),
            pltpu.VMEM((4 * BLOCK, 128), jnp.float32),
            pltpu.VMEM((points, width), jnp.bfloat16),
            pltpu.VMEM((rows, width), jnp.float32),
            pltpu.VMEM((rows, width), jnp.bfloat16),
            pltpu.VMEM((2, 2, HALO, width), jnp.bfloat16),
            pltpu.VMEM((2, HALO, width), jnp.bfloat16),
            pltpu.VMEM((2, HALO, width), jnp.bfloat16),
            pltpu.VMEM((2 * BLOCK, width), jnp.bfloat16),
            pltpu.VMEM((2, 1, BLOCK), jnp.int32),
            pltpu.SemaphoreType.DMA((8,)),
            pltpu.SemaphoreType.DMA((8,)),
        ],
        compiler_params=pltpu.CompilerParams(
            collective_id=0, has_side_effects=True, vmem_limit_bytes=48 * 1024 * 1024
        ),
        name="handover",
    )(
        places(m2g_src),
        places(mesh_src),
        state,
        mesh_latent,
        local_ids,
        lower_ids,
        upper_ids,
        norm_gain[:, None],
        w_dec_mesh,
        w_dec_grid,
        w_dec_out.T,
        w_enc,
        w_enc_out,
        w_proc_src,
        w_proc_dst,
        w_proc_out,
    )


def solution(mesh):
    placed = (
        P(None, ("groups", "band")),
        P(("groups", "band"), None),
        P(("groups", "band"), None),
        P(("groups", "band"), None),
        P(("groups", "band"), None),
        P(("groups", "band"), None),
        P(),
        P(),
        P(),
        P(),
        P(),
        P(),
        P(),
        P(),
        P(),
    )
    return jax.shard_map(
        functools.partial(shards, mesh.shape["band"]),
        mesh=mesh,
        in_specs=placed,
        out_specs=(P(None, ("groups", "band")), P(("groups", "band"), None)),
        check_vma=False,
    )
```

```python
import functools

import jax
import jax.numpy as jnp
from jax import lax
from jax.experimental import pallas as pl
from jax.experimental.pallas import tpu as pltpu
from jax.sharding import PartitionSpec as P

HALO = 128
KD = 3
KN = 6
BLOCK = 256
UNROLL = 16
PAD = 8


def dot(left, right, left_dim=1, right_dim=0):
    return lax.dot_general(
        left, right, (((left_dim,), (right_dim,)), ((), ())), preferred_element_type=jnp.float32
    )


def half_silu(half):
    return half * jnp.tanh(half) + half


def put_rows(table, first, values):
    count = values.shape[0]
    for part in range(values.shape[1] // 128):
        table[pl.ds(first + part, count, stride=4), :] = values[:, part * 128 : part * 128 + 128]


def get_rows(table, first, count):
    return jnp.concatenate(
        [table[pl.ds(first + part, count, stride=4), :] for part in range(4)], axis=1
    )


def gather_sum(table, index, rows, fanout, base, total, first):
    upper = lax.broadcasted_iota(jnp.int32, (8, 128), 0) >= 4

    def body(step, carry):
        point = pl.multiple_of(first + 2 * UNROLL * step, 2 * UNROLL)
        views = [
            index.at[pl.ds(edge * rows + point, 2 * UNROLL)] for edge in range(fanout)
        ]
        near = base.at[pl.ds(pl.multiple_of(4 * point, 8 * UNROLL), 8 * UNROLL)]
        far = total.at[pl.ds(pl.multiple_of(step * 8 * UNROLL, 8 * UNROLL), 8 * UNROLL)]
        for inner in range(UNROLL):
            spot = pl.ds(8 * inner, 8)
            own = near[spot, :]
            summed = None
            for edge in range(fanout):
                left = table[pl.ds(views[edge][2 * inner], 8), :]
                right = table[pl.ds(views[edge][2 * inner + 1], 8), :]
                term = half_silu(jnp.where(upper, right, left) + own)
                summed = term if summed is None else summed + term
            far[spot, :] = summed
        return carry

    lax.fori_loop(0, BLOCK // 2 // UNROLL, body, 0)


def one_hot(ids, first):
    rows = lax.broadcasted_iota(jnp.int32, (BLOCK, ids.shape[1]), 0) + first
    return jnp.where(rows == ids, 1.0, 0.0).astype(jnp.bfloat16)


def kernel(
    bands,
    m2g_index,
    mesh_index,
    owner,
    node,
    gain_row,
    far_state,
    far_latent,
    far_w_dec_mesh,
    far_w_dec_grid,
    far_w_dec_out,
    far_w_enc,
    far_w_enc_out,
    far_w_proc_src,
    far_w_proc_dst,
    far_w_proc_out,
    new_state,
    mesh_out,
    table,
    base,
    total,
    message,
    collected,
    middle,
    halo_out,
    halo_in,
    halo_in2,
    rim,
    rim_ids,
    send_sem,
    recv_sem,
    load_sem,
    window_ids,
    local_ids,
    gain,
    state,
    latent,
    w_dec_mesh,
    w_dec_grid,
    w_dec_out,
    w_enc,
    w_enc_out,
    w_proc_src,
    w_proc_dst,
    w_proc_out,
):
    me = lax.axis_index("band")
    rows = latent.shape[0]
    points = state.shape[1]
    blocks = rows // BLOCK
    has = (me > 0, me < bands - 1)
    other = (me - 1, me + 1)

    def copy(number, side, source, target):
        return pltpu.make_async_remote_copy(
            src_ref=source,
            dst_ref=target,
            send_sem=send_sem.at[2 * number + side],
            recv_sem=recv_sem.at[2 * number + side],
            device_id={"band": other[side]},
            device_id_type=pl.DeviceIdType.MESH,
        )

    def halo_copy(number, side, landing):
        return copy(number, side, halo_out.at[number // 3, side], landing.at[1 - side])

    def ids_copy(side):
        return copy(1, side, window_ids.at[side], rim_ids.at[1 - side])

    def rim_copy(side):
        start = 0 if side == 0 else points - BLOCK
        return copy(
            2, side, message.at[pl.ds(start, BLOCK)], rim.at[pl.ds((1 - side) * BLOCK, BLOCK)]
        )

    def start(make):
        for side in (0, 1):

            @pl.when(has[side])
            def _():
                make(side).start()

    def finish(make):
        for side in (0, 1):

            @pl.when(has[side])
            def _():
                make(side).wait_send()

            @pl.when(has[1 - side])
            def _():
                make(side).wait_recv()

    proj_copy = functools.partial(halo_copy, 0, landing=halo_in)
    send_copy = functools.partial(halo_copy, 3, landing=halo_in2)

    def block_of(step):
        return jnp.where(step == 0, 0, jnp.where(step == 1, blocks - 1, step - 1))

    def unpack(landing):
        for side in (0, 1):
            first = PAD + side * 4 * (HALO + rows)

            @pl.when(has[side])
            def _():
                put_rows(table, first, 0.5 * landing[side].astype(jnp.float32))

    def fill_block(step, source, weight, number):
        block = block_of(step)
        row = pl.multiple_of(block * BLOCK, BLOCK)
        values = dot(source[pl.ds(row, BLOCK), :], weight[...])
        put_rows(table, PAD + 4 * (HALO + row), 0.5 * values)
        return values

    middle_rows = rows - 2 * BLOCK

    def latent_part(first, count):
        return far_latent.at[pl.ds(first, count)], latent.at[pl.ds(first, count)]

    loads = dict(
        latent_first=latent_part(0, BLOCK),
        w_dec_mesh=(far_w_dec_mesh, w_dec_mesh),
        latent_last=latent_part(rows - BLOCK, BLOCK),
        latent_middle=latent_part(BLOCK, middle_rows),
        w_dec_grid=(far_w_dec_grid, w_dec_grid),
        state=(far_state, state),
        w_dec_out=(far_w_dec_out, w_dec_out),
        w_enc=(far_w_enc, w_enc),
        w_enc_out=(far_w_enc_out, w_enc_out),
        w_proc_src=(far_w_proc_src, w_proc_src),
        w_proc_dst=(far_w_proc_dst, w_proc_dst),
        w_proc_out=(far_w_proc_out, w_proc_out),
    )
    loads = {
        name: pltpu.make_async_copy(source, target, load_sem.at[number])
        for number, (name, (source, target)) in enumerate(loads.items())
    }
    for load in loads.values():
        load.start()

    barrier = pltpu.get_barrier_semaphore()
    for side in (0, 1):

        @pl.when(has[side])
        def _():
            pl.semaphore_signal(
                barrier,
                inc=1,
                device_id={"band": other[side]},
                device_id_type=pl.DeviceIdType.MESH,
            )

    pl.semaphore_wait(barrier, jnp.where(me > 0, 1, 0) + jnp.where(me < bands - 1, 1, 0))

    for side in (0, 1):

        @pl.when(jnp.logical_not(has[side]))
        def _():
            first = PAD + side * 4 * (HALO + rows)
            table[pl.ds(first, 4 * HALO), :] = jnp.zeros((4 * HALO, 128), jnp.float32)
            rim[pl.ds(side * BLOCK, BLOCK), :] = jnp.zeros((BLOCK, rim.shape[1]), rim.dtype)
            rim_ids[side] = jnp.full((1, BLOCK), -1, jnp.int32)

    relative = owner[...] - me
    local_ids[...] = jnp.where(relative == 0, node[...], -1)
    window_ids[0] = jnp.where(relative == -1, node[...], -1)[:, :BLOCK]
    window_ids[1] = jnp.where(relative == 1, node[...], -1)[:, points - BLOCK :]
    start(ids_copy)
    channels = gain_row.shape[1]
    square = (channels, channels)
    same = lax.broadcasted_iota(jnp.int32, square, 0) == lax.broadcasted_iota(jnp.int32, square, 1)
    gain[...] = jnp.sum(jnp.where(same, gain_row[...], 0.0), axis=1, keepdims=True)
    for name in ("latent_first", "w_dec_mesh", "latent_last"):
        loads[name].wait()

    def project(step, carry):
        values = fill_block(step, latent, w_dec_mesh, 0)

        @pl.when(step == 0)
        def _():
            halo_out[0, 0] = values[:HALO].astype(jnp.bfloat16)

        @pl.when(step == 1)
        def _():
            halo_out[0, 1] = values[BLOCK - HALO :].astype(jnp.bfloat16)
            start(proj_copy)
            loads["latent_middle"].wait()

        return carry

    lax.fori_loop(0, blocks, project, 0)
    for name in ("w_dec_grid", "state"):
        loads[name].wait()

    def receive(block, carry):
        point = pl.multiple_of(block * BLOCK, BLOCK)
        cells = state[:, pl.ds(point, BLOCK)].astype(jnp.bfloat16)
        put_rows(base, 4 * point, 0.5 * dot(cells, w_dec_grid[...], 0, 0))
        return carry

    lax.fori_loop(0, points // BLOCK, receive, 0)
    for name in ("w_dec_out", "w_enc"):
        loads[name].wait()
    finish(proj_copy)
    unpack(halo_in)

    def decode(step, carry):
        block = block_of(step)
        point = pl.multiple_of(block * BLOCK, BLOCK)
        columns = pl.ds(point, BLOCK)
        cells = state[:, columns]
        gather_sum(table, m2g_index, points, KD, base, total, point)
        decoded = get_rows(total, 0, BLOCK).astype(jnp.bfloat16)
        fresh = cells + dot(w_dec_out[...], decoded, 1, 1)
        new_state[:, columns] = fresh
        average = jnp.mean(fresh, axis=0, keepdims=True)
        centered = fresh - average
        variance = jnp.mean(centered * centered, axis=0, keepdims=True)
        normed = (centered * lax.rsqrt(variance + 1e-05) * gain[...]).astype(jnp.bfloat16)
        sent = half_silu(0.5 * dot(normed, w_enc[...], 0, 0))
        message[columns, :] = sent.astype(jnp.bfloat16)

        @pl.when(step == 1)
        def _():
            start(rim_copy)

        return carry

    lax.fori_loop(0, points // BLOCK, decode, 0)

    def collect(block, carry):
        row = pl.multiple_of(block * BLOCK, BLOCK)
        collected[pl.ds(row, BLOCK), :] = dot(one_hot(local_ids[...], row), message[...])
        return carry

    lax.fori_loop(0, blocks, collect, 0)
    for name in ("w_enc_out", "w_proc_src", "w_proc_dst", "w_proc_out"):
        loads[name].wait()
    finish(ids_copy)
    finish(rim_copy)

    def update(step, carry):
        block = block_of(step)
        row = pl.multiple_of(block * BLOCK, BLOCK)
        span = pl.ds(row, BLOCK)
        encoded = collected[span, :]
        for side in (0, 1):
            encoded += dot(one_hot(rim_ids[side], row), rim[pl.ds(side * BLOCK, BLOCK), :])
        mixed = latent[span, :].astype(jnp.float32) + dot(
            encoded.astype(jnp.bfloat16), w_enc_out[...]
        )
        middle[span, :] = mixed.astype(jnp.bfloat16)
        values = fill_block(step, middle, w_proc_src, 1)

        @pl.when(step == 0)
        def _():
            halo_out[1, 0] = values[:HALO].astype(jnp.bfloat16)

        @pl.when(step == 1)
        def _():
            halo_out[1, 1] = values[BLOCK - HALO :].astype(jnp.bfloat16)
            start(send_copy)

        put_rows(base, 4 * row, 0.5 * dot(middle[span, :], w_proc_dst[...]))
        return carry

    lax.fori_loop(0, blocks, update, 0)
    finish(send_copy)
    unpack(halo_in2)

    def process(block, carry):
        row = pl.multiple_of(block * BLOCK, BLOCK)
        span = pl.ds(row, BLOCK)
        gather_sum(table, mesh_index, rows, KN, base, total, row)
        edges = get_rows(total, 0, BLOCK).astype(jnp.bfloat16)
        result = middle[span, :].astype(jnp.float32) + dot(edges, w_proc_out[...])
        mesh_out[span, :] = result.astype(jnp.bfloat16)
        return carry

    lax.fori_loop(0, blocks, process, 0)


def shards(
    bands,
    state,
    mesh_latent,
    m2g_src,
    g2m_owner,
    g2m_node,
    mesh_src,
    norm_gain,
    w_dec_mesh,
    w_dec_grid,
    w_dec_out,
    w_enc,
    w_enc_out,
    w_proc_src,
    w_proc_dst,
    w_proc_out,
):
    position = lax.axis_index("band")
    rows, width = mesh_latent.shape
    points = state.shape[1]

    def places(sources):
        count = sources.shape[0]
        parity = lax.broadcasted_iota(jnp.int32, (1, count), 1) % 2
        local = sources.T - (position * rows - HALO)
        return (4 * local + (PAD - 4 * parity)).reshape(-1)

    vmem = pl.BlockSpec(memory_space=pltpu.VMEM)
    smem = pl.BlockSpec(memory_space=pltpu.SMEM)
    hbm = pl.BlockSpec(memory_space=pltpu.HBM)
    near = (
        state,
        mesh_latent,
        w_dec_mesh,
        w_dec_grid,
        w_dec_out.T,
        w_enc,
        w_enc_out,
        w_proc_src,
        w_proc_dst,
        w_proc_out,
    )
    return pl.pallas_call(
        functools.partial(kernel, bands),
        out_shape=(
            jax.ShapeDtypeStruct(state.shape, jnp.float32),
            jax.ShapeDtypeStruct(mesh_latent.shape, jnp.bfloat16),
        ),
        in_specs=[smem] * 2 + [vmem] * 3 + [hbm] * 10,
        out_specs=(vmem, vmem),
        scratch_shapes=[
            pltpu.VMEM((PAD + 4 * (rows + 2 * HALO) + 8, 128), jnp.float32),
            pltpu.VMEM((4 * points, 128), jnp.float32),
            pltpu.VMEM((4 * BLOCK, 128), jnp.float32),
            pltpu.VMEM((points, width), jnp.bfloat16),
            pltpu.VMEM((rows, width), jnp.float32),
            pltpu.VMEM((rows, width), jnp.bfloat16),
            pltpu.VMEM((2, 2, HALO, width), jnp.bfloat16),
            pltpu.VMEM((2, HALO, width), jnp.bfloat16),
            pltpu.VMEM((2, HALO, width), jnp.bfloat16),
            pltpu.VMEM((2 * BLOCK, width), jnp.bfloat16),
            pltpu.VMEM((2, 1, BLOCK), jnp.int32),
            pltpu.SemaphoreType.DMA((8,)),
            pltpu.SemaphoreType.DMA((8,)),
            pltpu.SemaphoreType.DMA((12,)),
            pltpu.VMEM((2, 1, BLOCK), jnp.int32),
            pltpu.VMEM((1, points), jnp.int32),
            pltpu.VMEM((state.shape[0], 1), jnp.float32),
            *[pltpu.VMEM(item.shape, item.dtype) for item in near],
        ],
        compiler_params=pltpu.CompilerParams(
            collective_id=0, has_side_effects=True, vmem_limit_bytes=63 * 1024 * 1024
        ),
        name="handover",
    )(
        places(m2g_src),
        places(mesh_src),
        g2m_owner.T,
        g2m_node.T,
        norm_gain[None, :],
        *near,
    )


def solution(mesh):
    placed = (
        P(None, ("groups", "band")),
        P(("groups", "band"), None),
        P(("groups", "band"), None),
        P(("groups", "band"), None),
        P(("groups", "band"), None),
        P(("groups", "band"), None),
        P(),
        P(),
        P(),
        P(),
        P(),
        P(),
        P(),
        P(),
        P(),
    )
    return jax.shard_map(
        functools.partial(shards, mesh.shape["band"]),
        mesh=mesh,
        in_specs=placed,
        out_specs=(P(None, ("groups", "band")), P(("groups", "band"), None)),
        check_vma=False,
    )
```

```python
import functools

import jax
import jax.numpy as jnp
from jax import lax
from jax.experimental import pallas as pl
from jax.experimental.pallas import tpu as pltpu
from jax.sharding import PartitionSpec as P

HALO = 128
KD = 3
KN = 6
BLOCK = 256
UNROLL = 16
PAD = 8


def dot(left, right, left_dim=1, right_dim=0):
    return lax.dot_general(
        left, right, (((left_dim,), (right_dim,)), ((), ())), preferred_element_type=jnp.float32
    )


def half_silu(half):
    return half * jnp.tanh(half) + half


def put_rows(table, first, values):
    count = values.shape[0]
    for part in range(values.shape[1] // 128):
        table[pl.ds(first + part, count, stride=4), :] = values[:, part * 128 : part * 128 + 128]


def get_rows(table, first, count):
    return jnp.concatenate(
        [table[pl.ds(first + part, count, stride=4), :] for part in range(4)], axis=1
    )


def gather_sum(table, index, fanout, base, total, first):
    upper = lax.broadcasted_iota(jnp.int32, (8, 128), 0) >= 4

    def body(step, carry):
        point = pl.multiple_of(first + 2 * UNROLL * step, 2 * UNROLL)
        views = [
            index.at[edge, 0, pl.ds(point, 2 * UNROLL)] for edge in range(fanout)
        ]
        near = base.at[pl.ds(pl.multiple_of(4 * point, 8 * UNROLL), 8 * UNROLL)]
        far = total.at[pl.ds(pl.multiple_of(step * 8 * UNROLL, 8 * UNROLL), 8 * UNROLL)]
        for inner in range(UNROLL):
            spot = pl.ds(8 * inner, 8)
            own = near[spot, :]
            summed = None
            for edge in range(fanout):
                left = table[pl.ds(views[edge][2 * inner], 8), :]
                right = table[pl.ds(views[edge][2 * inner + 1], 8), :]
                term = half_silu(jnp.where(upper, right, left) + own)
                summed = term if summed is None else summed + term
            far[spot, :] = summed
        return carry

    lax.fori_loop(0, BLOCK // 2 // UNROLL, body, 0)


def one_hot(ids, first):
    rows = lax.broadcasted_iota(jnp.int32, (BLOCK, ids.shape[1]), 0) + first
    return jnp.where(rows == ids, 1.0, 0.0).astype(jnp.bfloat16)


def kernel(
    bands,
    m2g_src,
    mesh_src,
    owner,
    node,
    gain_row,
    far_state,
    far_latent,
    far_w_dec_mesh,
    far_w_dec_grid,
    far_w_dec_out,
    far_w_enc,
    far_w_enc_out,
    far_w_proc_src,
    far_w_proc_dst,
    far_w_proc_out,
    new_state,
    mesh_out,
    table,
    base,
    total,
    message,
    collected,
    middle,
    halo_out,
    halo_in,
    halo_in2,
    rim,
    rim_ids,
    send_sem,
    recv_sem,
    load_sem,
    index_sem,
    m2g_place,
    mesh_place,
    m2g_index,
    mesh_index,
    window_ids,
    local_ids,
    gain,
    state,
    latent,
    w_dec_mesh,
    w_dec_grid,
    w_dec_out,
    w_enc,
    w_enc_out,
    w_proc_src,
    w_proc_dst,
    w_proc_out,
):
    me = lax.axis_index("band")
    rows = latent.shape[0]
    points = state.shape[1]
    blocks = rows // BLOCK
    has = (me > 0, me < bands - 1)
    other = (me - 1, me + 1)

    def copy(number, side, source, target):
        return pltpu.make_async_remote_copy(
            src_ref=source,
            dst_ref=target,
            send_sem=send_sem.at[2 * number + side],
            recv_sem=recv_sem.at[2 * number + side],
            device_id={"band": other[side]},
            device_id_type=pl.DeviceIdType.MESH,
        )

    def halo_copy(number, side, landing):
        return copy(number, side, halo_out.at[number // 3, side], landing.at[1 - side])

    def ids_copy(side):
        return copy(1, side, window_ids.at[side], rim_ids.at[1 - side])

    def rim_copy(side):
        start = 0 if side == 0 else points - BLOCK
        return copy(
            2, side, message.at[pl.ds(start, BLOCK)], rim.at[pl.ds((1 - side) * BLOCK, BLOCK)]
        )

    def start(make):
        for side in (0, 1):

            @pl.when(has[side])
            def _():
                make(side).start()

    def finish(make):
        for side in (0, 1):

            @pl.when(has[side])
            def _():
                make(side).wait_send()

            @pl.when(has[1 - side])
            def _():
                make(side).wait_recv()

    proj_copy = functools.partial(halo_copy, 0, landing=halo_in)
    send_copy = functools.partial(halo_copy, 3, landing=halo_in2)

    def block_of(step):
        return jnp.where(step == 0, 0, jnp.where(step == 1, blocks - 1, step - 1))

    def unpack(landing):
        for side in (0, 1):
            first = PAD + side * 4 * (HALO + rows)

            @pl.when(has[side])
            def _():
                put_rows(table, first, 0.5 * landing[side].astype(jnp.float32))

    def fill_block(step, source, weight, number):
        block = block_of(step)
        row = pl.multiple_of(block * BLOCK, BLOCK)
        values = dot(source[pl.ds(row, BLOCK), :], weight[...])
        put_rows(table, PAD + 4 * (HALO + row), 0.5 * values)
        return values

    middle_rows = rows - 2 * BLOCK

    def latent_part(first, count):
        return far_latent.at[pl.ds(first, count)], latent.at[pl.ds(first, count)]

    loads = dict(
        latent_first=latent_part(0, BLOCK),
        w_dec_mesh=(far_w_dec_mesh, w_dec_mesh),
        latent_last=latent_part(rows - BLOCK, BLOCK),
        latent_middle=latent_part(BLOCK, middle_rows),
        w_dec_grid=(far_w_dec_grid, w_dec_grid),
        state=(far_state, state),
        w_dec_out=(far_w_dec_out, w_dec_out),
        w_enc=(far_w_enc, w_enc),
        w_enc_out=(far_w_enc_out, w_enc_out),
        w_proc_src=(far_w_proc_src, w_proc_src),
        w_proc_dst=(far_w_proc_dst, w_proc_dst),
        w_proc_out=(far_w_proc_out, w_proc_out),
    )
    loads = {
        name: pltpu.make_async_copy(source, target, load_sem.at[number])
        for number, (name, (source, target)) in enumerate(loads.items())
    }
    for load in loads.values():
        load.start()

    barrier = pltpu.get_barrier_semaphore()
    for side in (0, 1):

        @pl.when(has[side])
        def _():
            pl.semaphore_signal(
                barrier,
                inc=1,
                device_id={"band": other[side]},
                device_id_type=pl.DeviceIdType.MESH,
            )

    pl.semaphore_wait(barrier, jnp.where(me > 0, 1, 0) + jnp.where(me < bands - 1, 1, 0))

    for side in (0, 1):

        @pl.when(jnp.logical_not(has[side]))
        def _():
            first = PAD + side * 4 * (HALO + rows)
            table[pl.ds(first, 4 * HALO), :] = jnp.zeros((4 * HALO, 128), jnp.float32)
            rim[pl.ds(side * BLOCK, BLOCK), :] = jnp.zeros((BLOCK, rim.shape[1]), rim.dtype)
            rim_ids[side] = jnp.full((1, BLOCK), -1, jnp.int32)

    parity = lax.broadcasted_iota(jnp.int32, (1, points), 1) % 2
    shift = PAD - 4 * parity
    span = rows + 2 * HALO
    moves = []
    for number, (sources, place, index) in enumerate(
        ((m2g_src, m2g_place, m2g_index), (mesh_src, mesh_place, mesh_index))
    ):
        for edge in range(sources.shape[0]):
            local = sources[edge : edge + 1, :] - (me * rows - HALO)
            place[edge] = 4 * jnp.clip(local, 0, span - 1) + shift
        moves.append(pltpu.make_async_copy(place, index, index_sem.at[number]))
        moves[-1].start()
    relative = owner[...] - me
    local_ids[...] = jnp.where(relative == 0, node[...], -1)
    window_ids[0] = jnp.where(relative == -1, node[...], -1)[:, :BLOCK]
    window_ids[1] = jnp.where(relative == 1, node[...], -1)[:, points - BLOCK :]
    start(ids_copy)
    channels = gain_row.shape[1]
    square = (channels, channels)
    same = lax.broadcasted_iota(jnp.int32, square, 0) == lax.broadcasted_iota(jnp.int32, square, 1)
    gain[...] = jnp.sum(jnp.where(same, gain_row[...], 0.0), axis=1, keepdims=True)
    for name in ("latent_first", "w_dec_mesh", "latent_last"):
        loads[name].wait()

    def project(step, carry):
        values = fill_block(step, latent, w_dec_mesh, 0)

        @pl.when(step == 0)
        def _():
            halo_out[0, 0] = values[:HALO].astype(jnp.bfloat16)

        @pl.when(step == 1)
        def _():
            halo_out[0, 1] = values[BLOCK - HALO :].astype(jnp.bfloat16)
            start(proj_copy)
            loads["latent_middle"].wait()

        return carry

    lax.fori_loop(0, blocks, project, 0)
    for name in ("w_dec_grid", "state"):
        loads[name].wait()

    def receive(block, carry):
        point = pl.multiple_of(block * BLOCK, BLOCK)
        cells = state[:, pl.ds(point, BLOCK)].astype(jnp.bfloat16)
        put_rows(base, 4 * point, 0.5 * dot(cells, w_dec_grid[...], 0, 0))
        return carry

    lax.fori_loop(0, points // BLOCK, receive, 0)
    for name in ("w_dec_out", "w_enc"):
        loads[name].wait()
    for move in moves:
        move.wait()
    finish(proj_copy)
    unpack(halo_in)

    def decode(step, carry):
        block = block_of(step)
        point = pl.multiple_of(block * BLOCK, BLOCK)
        columns = pl.ds(point, BLOCK)
        cells = state[:, columns]
        gather_sum(table, m2g_index, KD, base, total, point)
        decoded = get_rows(total, 0, BLOCK).astype(jnp.bfloat16)
        fresh = cells + dot(w_dec_out[...], decoded, 1, 1)
        new_state[:, columns] = fresh
        average = jnp.mean(fresh, axis=0, keepdims=True)
        centered = fresh - average
        variance = jnp.mean(centered * centered, axis=0, keepdims=True)
        normed = (centered * lax.rsqrt(variance + 1e-05) * gain[...]).astype(jnp.bfloat16)
        sent = half_silu(0.5 * dot(normed, w_enc[...], 0, 0))
        message[columns, :] = sent.astype(jnp.bfloat16)

        @pl.when(step == 1)
        def _():
            start(rim_copy)

        return carry

    lax.fori_loop(0, points // BLOCK, decode, 0)

    def collect(block, carry):
        row = pl.multiple_of(block * BLOCK, BLOCK)
        collected[pl.ds(row, BLOCK), :] = dot(one_hot(local_ids[...], row), message[...])
        return carry

    lax.fori_loop(0, blocks, collect, 0)
    for name in ("w_enc_out", "w_proc_src", "w_proc_dst", "w_proc_out"):
        loads[name].wait()
    finish(ids_copy)
    finish(rim_copy)

    def update(step, carry):
        block = block_of(step)
        row = pl.multiple_of(block * BLOCK, BLOCK)
        span = pl.ds(row, BLOCK)
        encoded = collected[span, :]
        for side in (0, 1):
            encoded += dot(one_hot(rim_ids[side], row), rim[pl.ds(side * BLOCK, BLOCK), :])
        mixed = latent[span, :].astype(jnp.float32) + dot(
            encoded.astype(jnp.bfloat16), w_enc_out[...]
        )
        middle[span, :] = mixed.astype(jnp.bfloat16)
        values = fill_block(step, middle, w_proc_src, 1)

        @pl.when(step == 0)
        def _():
            halo_out[1, 0] = values[:HALO].astype(jnp.bfloat16)

        @pl.when(step == 1)
        def _():
            halo_out[1, 1] = values[BLOCK - HALO :].astype(jnp.bfloat16)
            start(send_copy)

        put_rows(base, 4 * row, 0.5 * dot(middle[span, :], w_proc_dst[...]))
        return carry

    lax.fori_loop(0, blocks, update, 0)
    finish(send_copy)
    unpack(halo_in2)

    def process(block, carry):
        row = pl.multiple_of(block * BLOCK, BLOCK)
        span = pl.ds(row, BLOCK)
        gather_sum(table, mesh_index, KN, base, total, row)
        edges = get_rows(total, 0, BLOCK).astype(jnp.bfloat16)
        result = middle[span, :].astype(jnp.float32) + dot(edges, w_proc_out[...])
        mesh_out[span, :] = result.astype(jnp.bfloat16)
        return carry

    lax.fori_loop(0, blocks, process, 0)


def shards(
    bands,
    state,
    mesh_latent,
    m2g_src,
    g2m_owner,
    g2m_node,
    mesh_src,
    norm_gain,
    w_dec_mesh,
    w_dec_grid,
    w_dec_out,
    w_enc,
    w_enc_out,
    w_proc_src,
    w_proc_dst,
    w_proc_out,
):
    rows, width = mesh_latent.shape
    points = state.shape[1]
    vmem = pl.BlockSpec(memory_space=pltpu.VMEM)
    hbm = pl.BlockSpec(memory_space=pltpu.HBM)
    near = (
        state,
        mesh_latent,
        w_dec_mesh,
        w_dec_grid,
        w_dec_out.T,
        w_enc,
        w_enc_out,
        w_proc_src,
        w_proc_dst,
        w_proc_out,
    )
    return pl.pallas_call(
        functools.partial(kernel, bands),
        out_shape=(
            pltpu.VMEM(state.shape, jnp.float32),
            pltpu.VMEM(mesh_latent.shape, jnp.bfloat16),
        ),
        in_specs=[vmem] * 5 + [hbm] * 10,
        out_specs=(vmem, vmem),
        scratch_shapes=[
            pltpu.VMEM((PAD + 4 * (rows + 2 * HALO) + 8, 128), jnp.float32),
            pltpu.VMEM((4 * points, 128), jnp.float32),
            pltpu.VMEM((4 * BLOCK, 128), jnp.float32),
            pltpu.VMEM((points, width), jnp.bfloat16),
            pltpu.VMEM((rows, width), jnp.float32),
            pltpu.VMEM((rows, width), jnp.bfloat16),
            pltpu.VMEM((2, 2, HALO, width), jnp.bfloat16),
            pltpu.VMEM((2, HALO, width), jnp.bfloat16),
            pltpu.VMEM((2, HALO, width), jnp.bfloat16),
            pltpu.VMEM((2 * BLOCK, width), jnp.bfloat16),
            pltpu.VMEM((2, 1, BLOCK), jnp.int32),
            pltpu.SemaphoreType.DMA((8,)),
            pltpu.SemaphoreType.DMA((8,)),
            pltpu.SemaphoreType.DMA((12,)),
            pltpu.SemaphoreType.DMA((2,)),
            pltpu.VMEM((KD, 1, points), jnp.int32),
            pltpu.VMEM((KN, 1, rows), jnp.int32),
            pltpu.SMEM((KD, 1, points), jnp.int32),
            pltpu.SMEM((KN, 1, rows), jnp.int32),
            pltpu.VMEM((2, 1, BLOCK), jnp.int32),
            pltpu.VMEM((1, points), jnp.int32),
            pltpu.VMEM((state.shape[0], 1), jnp.float32),
            *[pltpu.VMEM(item.shape, item.dtype) for item in near],
        ],
        compiler_params=pltpu.CompilerParams(
            collective_id=0, has_side_effects=True, vmem_limit_bytes=60 * 1024 * 1024
        ),
        name="handover",
    )(
        m2g_src.T,
        mesh_src.T,
        g2m_owner.T,
        g2m_node.T,
        norm_gain[None, :],
        *near,
    )


def solution(mesh):
    placed = (
        P(None, ("groups", "band")),
        P(("groups", "band"), None),
        P(("groups", "band"), None),
        P(("groups", "band"), None),
        P(("groups", "band"), None),
        P(("groups", "band"), None),
        P(),
        P(),
        P(),
        P(),
        P(),
        P(),
        P(),
        P(),
        P(),
    )
    return jax.shard_map(
        functools.partial(shards, mesh.shape["band"]),
        mesh=mesh,
        in_specs=placed,
        out_specs=(P(None, ("groups", "band")), P(("groups", "band"), None)),
        check_vma=False,
    )
```

```python
import functools

import jax
import jax.numpy as jnp
from jax import lax
from jax.experimental import pallas as pl
from jax.experimental.pallas import tpu as pltpu
from jax.sharding import PartitionSpec as P

HALO = 128
KD = 3
KN = 6
BLOCK = 512
WINDOW = 256
UNROLL = 32
PAD = 8


def dot(left, right, left_dim=1, right_dim=0):
    return lax.dot_general(
        left, right, (((left_dim,), (right_dim,)), ((), ())), preferred_element_type=jnp.float32
    )


def half_silu(half):
    return half * jnp.tanh(half) + half


def put_rows(table, first, values):
    count = values.shape[0]
    for part in range(values.shape[1] // 128):
        table[pl.ds(first + part, count, stride=4), :] = values[:, part * 128 : part * 128 + 128]


def get_rows(table, first, count):
    return jnp.concatenate(
        [table[pl.ds(first + part, count, stride=4), :] for part in range(4)], axis=1
    )


def gather_sum(table, index, fanout, base, total, first):
    upper = lax.broadcasted_iota(jnp.int32, (8, 128), 0) >= 4

    def body(step, carry):
        point = pl.multiple_of(first + 2 * UNROLL * step, 2 * UNROLL)
        views = [
            index.at[edge, 0, pl.ds(point, 2 * UNROLL)] for edge in range(fanout)
        ]
        near = base.at[pl.ds(pl.multiple_of(4 * point, 8 * UNROLL), 8 * UNROLL)]
        far = total.at[pl.ds(pl.multiple_of(step * 8 * UNROLL, 8 * UNROLL), 8 * UNROLL)]
        for inner in range(UNROLL):
            spot = pl.ds(8 * inner, 8)
            own = near[spot, :]
            summed = None
            for edge in range(fanout):
                left = table[pl.ds(views[edge][2 * inner], 8), :]
                right = table[pl.ds(views[edge][2 * inner + 1], 8), :]
                term = half_silu(jnp.where(upper, right, left) + own)
                summed = term if summed is None else summed + term
            far[spot, :] = summed
        return carry

    lax.fori_loop(0, BLOCK // 2 // UNROLL, body, 0)


def one_hot(ids, first):
    rows = lax.broadcasted_iota(jnp.int32, (BLOCK, ids.shape[1]), 0) + first
    return jnp.where(rows == ids, 1.0, 0.0).astype(jnp.bfloat16)


def kernel(
    bands,
    m2g_src,
    mesh_src,
    owner,
    node,
    gain_row,
    far_state,
    far_latent,
    far_w_dec_mesh,
    far_w_dec_grid,
    far_w_dec_out,
    far_w_enc,
    far_w_enc_out,
    far_w_proc_src,
    far_w_proc_dst,
    far_w_proc_out,
    new_state,
    mesh_out,
    table,
    base,
    total,
    message,
    collected,
    middle,
    halo_out,
    halo_in,
    halo_in2,
    rim,
    rim_ids,
    send_sem,
    recv_sem,
    load_sem,
    index_sem,
    m2g_place,
    mesh_place,
    m2g_index,
    mesh_index,
    window_ids,
    local_ids,
    gain,
    state,
    latent,
    w_dec_mesh,
    w_dec_grid,
    w_dec_out,
    w_enc,
    w_enc_out,
    w_proc_src,
    w_proc_dst,
    w_proc_out,
):
    me = lax.axis_index("band")
    rows = latent.shape[0]
    points = state.shape[1]
    blocks = rows // BLOCK
    has = (me > 0, me < bands - 1)
    other = (me - 1, me + 1)

    def copy(number, side, source, target):
        return pltpu.make_async_remote_copy(
            src_ref=source,
            dst_ref=target,
            send_sem=send_sem.at[2 * number + side],
            recv_sem=recv_sem.at[2 * number + side],
            device_id={"band": other[side]},
            device_id_type=pl.DeviceIdType.MESH,
        )

    def halo_copy(number, side, landing):
        return copy(number, side, halo_out.at[number // 3, side], landing.at[1 - side])

    def ids_copy(side):
        return copy(1, side, window_ids.at[side], rim_ids.at[1 - side])

    def rim_copy(side):
        start = 0 if side == 0 else points - WINDOW
        return copy(
            2, side, message.at[pl.ds(start, WINDOW)], rim.at[pl.ds((1 - side) * WINDOW, WINDOW)]
        )

    def start(make):
        for side in (0, 1):

            @pl.when(has[side])
            def _():
                make(side).start()

    def finish(make):
        for side in (0, 1):

            @pl.when(has[side])
            def _():
                make(side).wait_send()

            @pl.when(has[1 - side])
            def _():
                make(side).wait_recv()

    proj_copy = functools.partial(halo_copy, 0, landing=halo_in)
    send_copy = functools.partial(halo_copy, 3, landing=halo_in2)

    def block_of(step):
        return jnp.where(step == 0, 0, jnp.where(step == 1, blocks - 1, step - 1))

    def unpack(landing):
        for side in (0, 1):
            first = PAD + side * 4 * (HALO + rows)

            @pl.when(has[side])
            def _():
                put_rows(table, first, 0.5 * landing[side].astype(jnp.float32))

    def fill_block(step, source, weight, number):
        block = block_of(step)
        row = pl.multiple_of(block * BLOCK, BLOCK)
        values = dot(source[pl.ds(row, BLOCK), :], weight[...])
        put_rows(table, PAD + 4 * (HALO + row), 0.5 * values)
        return values

    middle_rows = rows - 2 * BLOCK

    def latent_part(first, count):
        return far_latent.at[pl.ds(first, count)], latent.at[pl.ds(first, count)]

    loads = dict(
        latent_first=latent_part(0, BLOCK),
        w_dec_mesh=(far_w_dec_mesh, w_dec_mesh),
        latent_last=latent_part(rows - BLOCK, BLOCK),
        latent_middle=latent_part(BLOCK, middle_rows),
        w_dec_grid=(far_w_dec_grid, w_dec_grid),
        state=(far_state, state),
        w_dec_out=(far_w_dec_out, w_dec_out),
        w_enc=(far_w_enc, w_enc),
        w_enc_out=(far_w_enc_out, w_enc_out),
        w_proc_src=(far_w_proc_src, w_proc_src),
        w_proc_dst=(far_w_proc_dst, w_proc_dst),
        w_proc_out=(far_w_proc_out, w_proc_out),
    )
    loads = {
        name: pltpu.make_async_copy(source, target, load_sem.at[number])
        for number, (name, (source, target)) in enumerate(loads.items())
    }
    for load in loads.values():
        load.start()

    barrier = pltpu.get_barrier_semaphore()
    for side in (0, 1):

        @pl.when(has[side])
        def _():
            pl.semaphore_signal(
                barrier,
                inc=1,
                device_id={"band": other[side]},
                device_id_type=pl.DeviceIdType.MESH,
            )

    pl.semaphore_wait(barrier, jnp.where(me > 0, 1, 0) + jnp.where(me < bands - 1, 1, 0))

    for side in (0, 1):

        @pl.when(jnp.logical_not(has[side]))
        def _():
            first = PAD + side * 4 * (HALO + rows)
            table[pl.ds(first, 4 * HALO), :] = jnp.zeros((4 * HALO, 128), jnp.float32)
            rim[pl.ds(side * WINDOW, WINDOW), :] = jnp.zeros((WINDOW, rim.shape[1]), rim.dtype)
            rim_ids[side] = jnp.full((1, WINDOW), -1, jnp.int32)

    parity = lax.broadcasted_iota(jnp.int32, (1, points), 1) % 2
    shift = PAD - 4 * parity
    span = rows + 2 * HALO
    moves = []
    for number, (sources, place, index) in enumerate(
        ((m2g_src, m2g_place, m2g_index), (mesh_src, mesh_place, mesh_index))
    ):
        for edge in range(sources.shape[0]):
            local = sources[edge : edge + 1, :] - (me * rows - HALO)
            place[edge] = 4 * jnp.clip(local, 0, span - 1) + shift
        moves.append(pltpu.make_async_copy(place, index, index_sem.at[number]))
        moves[-1].start()
    relative = owner[...] - me
    local_ids[...] = jnp.where(relative == 0, node[...], -1)
    window_ids[0] = jnp.where(relative == -1, node[...], -1)[:, :WINDOW]
    window_ids[1] = jnp.where(relative == 1, node[...], -1)[:, points - WINDOW :]
    start(ids_copy)
    channels = gain_row.shape[1]
    square = (channels, channels)
    same = lax.broadcasted_iota(jnp.int32, square, 0) == lax.broadcasted_iota(jnp.int32, square, 1)
    gain[...] = jnp.sum(jnp.where(same, gain_row[...], 0.0), axis=1, keepdims=True)
    for name in ("latent_first", "w_dec_mesh", "latent_last"):
        loads[name].wait()

    def project(step, carry):
        values = fill_block(step, latent, w_dec_mesh, 0)

        @pl.when(step == 0)
        def _():
            halo_out[0, 0] = values[:HALO].astype(jnp.bfloat16)

        @pl.when(step == 1)
        def _():
            halo_out[0, 1] = values[BLOCK - HALO :].astype(jnp.bfloat16)
            start(proj_copy)
            loads["latent_middle"].wait()

        return carry

    lax.fori_loop(0, blocks, project, 0)
    for name in ("w_dec_grid", "state"):
        loads[name].wait()

    def receive(block, carry):
        point = pl.multiple_of(block * BLOCK, BLOCK)
        cells = state[:, pl.ds(point, BLOCK)].astype(jnp.bfloat16)
        put_rows(base, 4 * point, 0.5 * dot(cells, w_dec_grid[...], 0, 0))
        return carry

    lax.fori_loop(0, points // BLOCK, receive, 0)
    for name in ("w_dec_out", "w_enc"):
        loads[name].wait()
    for move in moves:
        move.wait()
    finish(proj_copy)
    unpack(halo_in)

    def decode(step, carry):
        block = block_of(step)
        point = pl.multiple_of(block * BLOCK, BLOCK)
        columns = pl.ds(point, BLOCK)
        cells = state[:, columns]
        gather_sum(table, m2g_index, KD, base, total, point)
        decoded = get_rows(total, 0, BLOCK).astype(jnp.bfloat16)
        fresh = cells + dot(w_dec_out[...], decoded, 1, 1)
        new_state[:, columns] = fresh
        average = jnp.mean(fresh, axis=0, keepdims=True)
        centered = fresh - average
        variance = jnp.mean(centered * centered, axis=0, keepdims=True)
        normed = (centered * lax.rsqrt(variance + 1e-05) * gain[...]).astype(jnp.bfloat16)
        sent = half_silu(0.5 * dot(normed, w_enc[...], 0, 0))
        message[columns, :] = sent.astype(jnp.bfloat16)

        @pl.when(step == 1)
        def _():
            start(rim_copy)

        return carry

    lax.fori_loop(0, points // BLOCK, decode, 0)

    def collect(block, carry):
        row = pl.multiple_of(block * BLOCK, BLOCK)
        collected[pl.ds(row, BLOCK), :] = dot(one_hot(local_ids[...], row), message[...])
        return carry

    lax.fori_loop(0, blocks, collect, 0)
    for name in ("w_enc_out", "w_proc_src", "w_proc_dst", "w_proc_out"):
        loads[name].wait()
    finish(ids_copy)
    finish(rim_copy)

    def update(step, carry):
        block = block_of(step)
        row = pl.multiple_of(block * BLOCK, BLOCK)
        span = pl.ds(row, BLOCK)
        encoded = collected[span, :]
        for side in (0, 1):
            encoded += dot(one_hot(rim_ids[side], row), rim[pl.ds(side * WINDOW, WINDOW), :])
        mixed = latent[span, :].astype(jnp.float32) + dot(
            encoded.astype(jnp.bfloat16), w_enc_out[...]
        )
        middle[span, :] = mixed.astype(jnp.bfloat16)
        values = fill_block(step, middle, w_proc_src, 1)

        @pl.when(step == 0)
        def _():
            halo_out[1, 0] = values[:HALO].astype(jnp.bfloat16)

        @pl.when(step == 1)
        def _():
            halo_out[1, 1] = values[BLOCK - HALO :].astype(jnp.bfloat16)
            start(send_copy)

        put_rows(base, 4 * row, 0.5 * dot(middle[span, :], w_proc_dst[...]))
        return carry

    lax.fori_loop(0, blocks, update, 0)
    finish(send_copy)
    unpack(halo_in2)

    def process(block, carry):
        row = pl.multiple_of(block * BLOCK, BLOCK)
        span = pl.ds(row, BLOCK)
        gather_sum(table, mesh_index, KN, base, total, row)
        edges = get_rows(total, 0, BLOCK).astype(jnp.bfloat16)
        result = middle[span, :].astype(jnp.float32) + dot(edges, w_proc_out[...])
        mesh_out[span, :] = result.astype(jnp.bfloat16)
        return carry

    lax.fori_loop(0, blocks, process, 0)


def shards(
    bands,
    state,
    mesh_latent,
    m2g_src,
    g2m_owner,
    g2m_node,
    mesh_src,
    norm_gain,
    w_dec_mesh,
    w_dec_grid,
    w_dec_out,
    w_enc,
    w_enc_out,
    w_proc_src,
    w_proc_dst,
    w_proc_out,
):
    rows, width = mesh_latent.shape
    points = state.shape[1]
    vmem = pl.BlockSpec(memory_space=pltpu.VMEM)
    hbm = pl.BlockSpec(memory_space=pltpu.HBM)
    near = (
        state,
        mesh_latent,
        w_dec_mesh,
        w_dec_grid,
        w_dec_out.T,
        w_enc,
        w_enc_out,
        w_proc_src,
        w_proc_dst,
        w_proc_out,
    )
    return pl.pallas_call(
        functools.partial(kernel, bands),
        out_shape=(
            pltpu.VMEM(state.shape, jnp.float32),
            pltpu.VMEM(mesh_latent.shape, jnp.bfloat16),
        ),
        in_specs=[vmem] * 5 + [hbm] * 10,
        out_specs=(vmem, vmem),
        scratch_shapes=[
            pltpu.VMEM((PAD + 4 * (rows + 2 * HALO) + 8, 128), jnp.float32),
            pltpu.VMEM((4 * points, 128), jnp.float32),
            pltpu.VMEM((4 * BLOCK, 128), jnp.float32),
            pltpu.VMEM((points, width), jnp.bfloat16),
            pltpu.VMEM((rows, width), jnp.float32),
            pltpu.VMEM((rows, width), jnp.bfloat16),
            pltpu.VMEM((2, 2, HALO, width), jnp.bfloat16),
            pltpu.VMEM((2, HALO, width), jnp.bfloat16),
            pltpu.VMEM((2, HALO, width), jnp.bfloat16),
            pltpu.VMEM((2 * WINDOW, width), jnp.bfloat16),
            pltpu.VMEM((2, 1, WINDOW), jnp.int32),
            pltpu.SemaphoreType.DMA((8,)),
            pltpu.SemaphoreType.DMA((8,)),
            pltpu.SemaphoreType.DMA((12,)),
            pltpu.SemaphoreType.DMA((2,)),
            pltpu.VMEM((KD, 1, points), jnp.int32),
            pltpu.VMEM((KN, 1, rows), jnp.int32),
            pltpu.SMEM((KD, 1, points), jnp.int32),
            pltpu.SMEM((KN, 1, rows), jnp.int32),
            pltpu.VMEM((2, 1, WINDOW), jnp.int32),
            pltpu.VMEM((1, points), jnp.int32),
            pltpu.VMEM((state.shape[0], 1), jnp.float32),
            *[pltpu.VMEM(item.shape, item.dtype) for item in near],
        ],
        compiler_params=pltpu.CompilerParams(
            collective_id=0, has_side_effects=True, vmem_limit_bytes=60 * 1024 * 1024
        ),
        name="handover",
    )(
        m2g_src.T,
        mesh_src.T,
        g2m_owner.T,
        g2m_node.T,
        norm_gain[None, :],
        *near,
    )


def solution(mesh):
    placed = (
        P(None, ("groups", "band")),
        P(("groups", "band"), None),
        P(("groups", "band"), None),
        P(("groups", "band"), None),
        P(("groups", "band"), None),
        P(("groups", "band"), None),
        P(),
        P(),
        P(),
        P(),
        P(),
        P(),
        P(),
        P(),
        P(),
    )
    return jax.shard_map(
        functools.partial(shards, mesh.shape["band"]),
        mesh=mesh,
        in_specs=placed,
        out_specs=(P(None, ("groups", "band")), P(("groups", "band"), None)),
        check_vma=False,
    )
```
